512 devices in a mesh: dp: 8 (over x, core), row: 8 (over y, z_hi), col: 8 (over z_lo).
Axes of the slice: x: 4, y: 4, z: 16 (z_hi: 2, z_lo: 8; z = z_hi * 8 + z_lo), core: 2. Of those that a mesh axis runs over, the one named last changes fastest.
Arguments:
- activations: bfloat16 [384, 8192], P(('dp', 'col'), 'row'), may hold values from -6 to 6
- gate_weight: bfloat16 [8192, 24576], P('row', ('dp', 'col')), may hold values from -0.0625 to 0.0625
- up_weight: bfloat16 [8192, 24576], P('row', ('dp', 'col')), may hold values from -0.0625 to 0.0625
- down_weight: bfloat16 [24576, 8192], P(('dp', 'col'), 'row'), may hold values from -0.0390625 to 0.0390625
- output_cotangent: bfloat16 [384, 8192], P(('dp', 'col'), 'row'), may hold values from -6 to 6
Outputs:
- layer_output: bfloat16 [384, 8192], P(('dp', 'col'), 'row')
- input_gradient: bfloat16 [384, 8192], P(('dp', 'col'), 'row')
- gate_gradient: bfloat16 [8192, 24576], P('row', ('dp', 'col'))
- up_gradient: bfloat16 [8192, 24576], P('row', ('dp', 'col'))
- down_gradient: bfloat16 [24576, 8192], P(('dp', 'col'), 'row')
The draws below stay inside these ranges and needn't reach their ends.
All inputs are finite; a program needn't handle non-finite values.
Results may differ from the reference program's by a relative error of at most 0.029.
Values may be sent and summed in bfloat16 or wider, within the bound.
A program may use at most 64 MiB of HBM per device.

```python
import jax
import jax.numpy as jnp
from jax import lax

D = 8192
FF = 24576
TOKENS = 384
N_ROW = 8


def level_of(rng, dims, split, smallest, high):
    level = 1.0
    for dim, blocks in split:
        draws = jax.random.uniform(jax.random.fold_in(jax.random.fold_in(rng, 6), dim), (blocks,), jnp.float32, smallest / len(split), high / len(split))
        level = level * jnp.repeat(jnp.exp(draws), dims[dim] // blocks).reshape((-1,) + (1,) * (len(dims) - 1 - dim))
    return level


def scatter_about(own_key, extent, deviation, bound, pieces=(), kind=jnp.bfloat16):
    values = jax.random.normal(own_key, extent, jnp.float32) * deviation
    if len(pieces) > 0:
        values = level_of(own_key, extent, pieces, -0.22, 0.18) * values
    return jnp.clip(values, min=-bound, max=bound).astype(kind)


def setup_inputs(seed: int = 0) -> dict:
    streams_of = jax.random.split(jax.random.key(seed), 6)
    activations = scatter_about(streams_of[0], (TOKENS, D), 1.0, 6.0, ((0, 64), (1, 8)))
    gate_weight = scatter_about(streams_of[1], (D, FF), D ** -0.5, 0.0625, ((0, 8), (1, 64)))
    up_weight = scatter_about(streams_of[2], (D, FF), D ** -0.5, 0.0625, ((0, 8), (1, 64)))
    down_weight = scatter_about(streams_of[3], (FF, D), FF ** -0.5, 0.0390625, ((0, 64), (1, 8)))
    output_cotangent = scatter_about(streams_of[4], (TOKENS, D), 1.0, 6.0, ((0, 64), (1, 8)))
    return {"activations": activations, "gate_weight": gate_weight, "up_weight": up_weight, "down_weight": down_weight, "output_cotangent": output_cotangent}


def rounded(value):
    return lax.optimization_barrier(value.astype(jnp.bfloat16)).astype(jnp.float32)


def block_sum(left_side, right_side, blocks, contract_last):
    block_width = left_side.shape[1] // blocks
    out_width = right_side.shape[0] if contract_last else right_side.shape[1]
    running_total = jnp.zeros((left_side.shape[0], out_width), jnp.float32)
    for block_index in range(blocks):
        left_piece = left_side[:, block_index * block_width:(block_index + 1) * block_width]
        if contract_last:
            right_piece = right_side[:, block_index * block_width:(block_index + 1) * block_width]
            product = lax.dot_general(left_piece, right_piece, (((1,), (1,)), ((), ())), preferred_element_type=jnp.float32)
        else:
            right_piece = right_side[block_index * block_width:(block_index + 1) * block_width, :]
            product = jnp.dot(left_piece, right_piece, preferred_element_type=jnp.float32)
        running_total = running_total + rounded(product)
    return running_total


def reference(activations, gate_weight, up_weight, down_weight, output_cotangent):
    gate_sum = block_sum(activations, gate_weight, N_ROW, False)
    up_sum = block_sum(activations, up_weight, N_ROW, False)
    sigmoid = jax.nn.sigmoid(gate_sum)
    hidden = (gate_sum * sigmoid * up_sum).astype(jnp.bfloat16)
    layer_output = jnp.dot(hidden, down_weight, preferred_element_type=jnp.float32).astype(jnp.bfloat16)
    hidden_slope = block_sum(output_cotangent, down_weight, N_ROW, True)
    gate_slope = (hidden_slope * up_sum * sigmoid * (1.0 + gate_sum * (1.0 - sigmoid))).astype(jnp.bfloat16)
    up_slope = (hidden_slope * gate_sum * sigmoid).astype(jnp.bfloat16)
    along_hidden = (((1,), (1,)), ((), ()))
    along_tokens = (((0,), (0,)), ((), ()))
    input_total = lax.dot_general(gate_slope, gate_weight, along_hidden, preferred_element_type=jnp.float32)
    input_total = input_total + lax.dot_general(up_slope, up_weight, along_hidden, preferred_element_type=jnp.float32)
    input_gradient = input_total.astype(jnp.bfloat16)
    gate_gradient = lax.dot_general(activations, gate_slope, along_tokens, preferred_element_type=jnp.float32).astype(jnp.bfloat16)
    up_gradient = lax.dot_general(activations, up_slope, along_tokens, preferred_element_type=jnp.float32).astype(jnp.bfloat16)
    down_gradient = lax.dot_general(hidden, output_cotangent, along_tokens, preferred_element_type=jnp.float32).astype(jnp.bfloat16)
    return layer_output, input_gradient, gate_gradient, up_gradient, down_gradient
```

```python
import jax
import jax.numpy as jnp
from jax import lax
from jax.experimental import pallas as pl
from jax.experimental.pallas import tpu as pltpu
from jax.sharding import PartitionSpec as P

MESH = pl.DeviceIdType.MESH
F32 = jnp.float32
BF16 = jnp.bfloat16
LANES = 128
OWN = 6
NX, NY, NZ = 4, 4, 8
BLOCK = OWN * NZ
HALF = NX * BLOCK
WIDTH = 1024
HID = 384
CHUNKS = WIDTH // LANES


def dot(left, right, dims):
    return lax.dot_general(left, right, (dims, ((), ())), preferred_element_type=F32)


def over_tokens(left, right):
    left, right = (v.reshape(2 * HALF, v.shape[-1]) for v in (left, right))
    return dot(left, right, ((0,), (0,))).astype(BF16)


def kernel(
    act_ref, cot_ref, gw_hbm, uw_hbm, dw_hbm,
    out_ref, inp_ref, gg_hbm, ug_hbm, dg_hbm,
    wgu, wd, zpiece, xall,
    gpart, grecv, gsend, gz, spart, srecv, ssend, sz, sums,
    hid, slope, part, crecv, xsend, xrecv, zsend, zrecv, gradg, gradu, gradd,
    wsem, osem,
    z_s, z_r, x_s, x_r, c_s, c_r, yg_s, yg_r, ys_s, ys_r, e_s, e_r,
    yh_s, yh_r, yl_s, yl_r, fc_s, fc_r, fx_s, fx_r, fz_s, fz_r,
):
    dp, row, zl = lax.axis_index("dp"), lax.axis_index("row"), lax.axis_index("col")
    x, c = dp // 2, lax.rem(dp, 2)
    y, zh = row // 2, lax.rem(row, 2)

    sib = {"dp": x * 2 + 1 - c}
    far = {"row": y * 2 + 1 - zh}

    def xpos(i):
        return lax.rem(x + i, NX)

    def ypos(i):
        return lax.rem(y + i, NY)

    def zpos(i):
        return lax.rem(zl + i, NZ)

    def xdev(i):
        return {"dp": xpos(i) * 2 + c}

    def ydev(i):
        return {"row": ypos(i) * 2 + zh}

    def zdev(i):
        return {"col": zpos(i)}

    loads = [
        pltpu.make_async_copy(gw_hbm, wgu.at[:, 0:HID], wsem.at[0]),
        pltpu.make_async_copy(uw_hbm, wgu.at[:, HID : 2 * HID], wsem.at[1]),
        pltpu.make_async_copy(dw_hbm, wd, wsem.at[2]),
    ]
    for load in loads:
        load.start()

    barrier = pltpu.get_barrier_semaphore()
    peers = [sib, far]
    peers += [xdev(i) for i in range(1, NX)]
    peers += [ydev(i) for i in range(1, NY)]
    peers += [zdev(i) for i in range(1, NZ)]
    for peer in peers:
        pl.semaphore_signal(barrier, inc=1, device_id=peer, device_id_type=MESH)

    def to_fine(value):
        return value.reshape(value.shape[0] * CHUNKS, LANES)

    def from_fine(value):
        return value.reshape(value.shape[0] // CHUNKS, WIDTH)

    for kind, ref in ((0, act_ref), (1, cot_ref)):
        zpiece[kind, zl] = to_fine(ref[...].astype(F32)).astype(BF16)

    pl.semaphore_wait(barrier, len(peers))

    started = []

    def send(src, dst, s, r, device):
        copy = pltpu.make_async_remote_copy(
            src_ref=src, dst_ref=dst, send_sem=s, recv_sem=r, device_id=device, device_id_type=MESH
        )
        copy.start()
        started.append(copy)
        return copy

    def z_gather(kind):
        return [
            send(zpiece.at[kind, zl], zpiece.at[kind, zl], z_s.at[kind, i], z_r.at[kind, i], zdev(i + 1))
            for i in range(NZ - 1)
        ]

    def forward(kind, where, i):
        block = xall.at[kind, c, where]
        return send(block, block, c_s.at[kind, i], c_r.at[kind, i], sib)

    def x_gather(kind, copies):
        for copy in copies:
            copy.wait_recv()
        pieces = zpiece[kind].reshape(NZ * OWN * CHUNKS, LANES).astype(F32)
        xall[kind, c, x] = from_fine(pieces).astype(BF16)
        block = xall.at[kind, c, x]
        xs = [
            send(block, block, x_s.at[kind, i], x_r.at[kind, i], xdev(i + 1))
            for i in range(NX - 1)
        ]
        return xs, [forward(kind, x, 0)]

    def pass_on(kind, xs, cs):
        for i in (0, 2, 1):
            xs[i].wait_recv()
            cs.append(forward(kind, lax.rem(x + NX - i - 1, NX), i + 1))

    def y_scatter(t, parts, recv, s, r):
        return [
            send(parts.at[t, ypos(i + 1)], recv.at[t, i], s.at[t, i], r.at[t, i], ydev(i + 1))
            for i in range(NY - 1)
        ]

    def y_gather(t, buf, s, r):
        return [
            send(buf.at[t, y], buf.at[t, y], s.at[t, i], r.at[t, i], ydev(i + 1))
            for i in range(NY - 1)
        ]

    def y_sum(t, copies, parts, recv, out):
        total = parts[t, y].astype(F32)
        for i in (0, 2, 1):
            copies[i].wait_recv()
            total = total + recv[t, i].astype(F32)
        out[t] = total.astype(BF16)

    def received(copies):
        for copy in copies:
            copy.wait_recv()

    az = z_gather(0)
    ax, ac = x_gather(0, az)
    cz = z_gather(1)
    pass_on(0, ax, ac)
    loads[0].wait()
    loads[1].wait()
    received(ac)

    yg = []
    for t in range(2):
        gpart[t] = (
            dot(xall[0, t].reshape(HALF, WIDTH), wgu[...], ((1,), (0,)))
            .astype(BF16)
            .reshape(NY, BLOCK, 2 * HID)
        )
        yg.append(y_scatter(t, gpart, grecv, yg_s, yg_r))

    eg = []

    def exchange(t, k, src, dst):
        return send(src.at[t], dst.at[t], e_s.at[k, t], e_r.at[k, t], far)

    cx, cc = x_gather(1, cz)
    y_sum(0, yg[0], gpart, grecv, gsend)
    eg.append(exchange(0, 0, gsend, gz))
    pass_on(1, cx, cc)
    y_sum(1, yg[1], gpart, grecv, gsend)
    eg.append(exchange(1, 0, gsend, gz))
    loads[2].wait()
    received(cc)

    ys, es = [], []
    for t in range(2):
        spart[t] = (
            dot(xall[1, t].reshape(HALF, WIDTH), wd[...], ((1,), (1,)))
            .astype(BF16)
            .reshape(NY, BLOCK, HID)
        )
        ys.append(y_scatter(t, spart, srecv, ys_s, ys_r))
    for t in range(2):
        y_sum(t, ys[t], spart, srecv, ssend)
        es.append(exchange(t, 1, ssend, sz))

    yh = []
    for t in range(2):
        eg[t].wait_recv()
        both = gsend[t].astype(F32) + gz[t].astype(F32)
        sums[t] = both
        gate, up = both[:, 0:HID], both[:, HID : 2 * HID]
        hid[t, y] = (gate * jax.nn.sigmoid(gate) * up).astype(BF16)
        yh.append(y_gather(t, hid, yh_s, yh_r))

    def scatter_core(k, t):
        return pltpu.make_async_remote_copy(
            src_ref=part.at[k, t], dst_ref=crecv.at[k], send_sem=fc_s.at[k],
            recv_sem=fc_r.at[k], device_id=sib, device_id_type=MESH,
        )

    def scatter_x(k):
        scatter_core(k, 1 - c).wait_recv()
        xsend[k] = (part[k, c].astype(F32) + crecv[k].astype(F32)).astype(BF16)
        return [
            send(xsend.at[k, xpos(i + 1)], xrecv.at[k, i], fx_s.at[k, i], fx_r.at[k, i], xdev(i + 1))
            for i in range(NX - 1)
        ]

    def scatter_z(k, copies):
        total = xsend[k, x].astype(F32)
        for i in (0, 2, 1):
            copies[i].wait_recv()
            total = total + xrecv[k, i].astype(F32)
        zsend[k] = to_fine(total).astype(BF16).reshape(NZ, OWN * CHUNKS, LANES)
        return [
            send(zsend.at[k, zpos(i + 1)], zrecv.at[k, i], fz_s.at[k, i], fz_r.at[k, i], zdev(i + 1))
            for i in range(NZ - 1)
        ]

    def finish(k, copies, ref):
        total = zsend[k, zl].astype(F32)
        for i in range(NZ - 1):
            copies[i].wait_recv()
            total = total + zrecv[k, i].astype(F32)
        ref[...] = from_fine(total).astype(BF16)

    for t in range(2):
        received(yh[t])
        part[0, t] = (
            dot(hid[t].reshape(HALF, HID), wd[...], ((1,), (0,))).astype(BF16).reshape(NX, BLOCK, WIDTH)
        )
    scatter_core(0, 1 - c).start()
    fx_o = scatter_x(0)
    cots = xall.at[1]

    @pl.loop(0, HID // LANES)
    def _(j):
        at = pl.ds(pl.multiple_of(j * LANES, LANES), LANES)
        gradd[at, :] = over_tokens(hid[:, :, :, at], cots[...])

    stores = [pltpu.make_async_copy(gradd, dg_hbm, osem.at[0])]
    stores[0].start()

    yl = []
    for t in range(2):
        es[t].wait_recv()
        both = sums[t]
        gate, up = both[:, 0:HID], both[:, HID : 2 * HID]
        ds = ssend[t].astype(F32) + sz[t].astype(F32)
        s = jax.nn.sigmoid(gate)
        slope[t, y, :, 0:HID] = (ds * up * s * (1.0 + gate * (1.0 - s))).astype(BF16)
        slope[t, y, :, HID : 2 * HID] = (ds * gate * s).astype(BF16)
        yl.append(y_gather(t, slope, yl_s, yl_r))
        if t == 0:
            fz_o = scatter_z(0, fx_o)

    for t in range(2):
        received(yl[t])
        part[1, t] = (
            dot(slope[t].reshape(HALF, 2 * HID), wgu[...], ((1,), (1,)))
            .astype(BF16)
            .reshape(NX, BLOCK, WIDTH)
        )

        @pl.when(c == 1 - t)
        def _():
            scatter_core(1, t).start()

        if t == 0:
            finish(0, fz_o, out_ref)

    fx_i = scatter_x(1)

    @pl.loop(0, CHUNKS)
    def _(j):
        at = pl.ds(pl.multiple_of(j * LANES, LANES), LANES)
        gradg[at, :] = over_tokens(xall[0, :, :, :, at], slope[:, :, :, 0:HID])

    stores.append(pltpu.make_async_copy(gradg, gg_hbm, osem.at[1]))
    stores[1].start()
    fz_i = scatter_z(1, fx_i)

    @pl.loop(0, CHUNKS)
    def _(j):
        at = pl.ds(pl.multiple_of(j * LANES, LANES), LANES)
        gradu[at, :] = over_tokens(xall[0, :, :, :, at], slope[:, :, :, HID : 2 * HID])

    stores.append(pltpu.make_async_copy(gradu, ug_hbm, osem.at[2]))
    stores[2].start()
    finish(1, fz_i, inp_ref)
    for k in range(2):
        scatter_core(k, 1 - c).wait_send()
    for copy in started:
        copy.wait_send()
    for store in stores:
        store.wait()


def body(activations, gate_weight, up_weight, down_weight, output_cotangent):
    vmem = pl.BlockSpec(memory_space=pltpu.VMEM)
    hbm = pl.BlockSpec(memory_space=pl.ANY)
    dma = pltpu.SemaphoreType.DMA
    small = jax.ShapeDtypeStruct((OWN, WIDTH), BF16)
    tall = jax.ShapeDtypeStruct((WIDTH, HID), BF16)
    scratch = [
        pltpu.VMEM((WIDTH, 2 * HID), BF16),
        pltpu.VMEM((HID, WIDTH), BF16),
        pltpu.VMEM((2, NZ, OWN * CHUNKS, LANES), BF16),
        pltpu.VMEM((2, 2, NX, BLOCK, WIDTH), BF16),
        pltpu.VMEM((2, NY, BLOCK, 2 * HID), BF16),
        pltpu.VMEM((2, NY - 1, BLOCK, 2 * HID), BF16),
        pltpu.VMEM((2, BLOCK, 2 * HID), BF16),
        pltpu.VMEM((2, BLOCK, 2 * HID), BF16),
        pltpu.VMEM((2, NY, BLOCK, HID), BF16),
        pltpu.VMEM((2, NY - 1, BLOCK, HID), BF16),
        pltpu.VMEM((2, BLOCK, HID), BF16),
        pltpu.VMEM((2, BLOCK, HID), BF16),
        pltpu.VMEM((2, BLOCK, 2 * HID), F32),
        pltpu.VMEM((2, NY, BLOCK, HID), BF16),
        pltpu.VMEM((2, NY, BLOCK, 2 * HID), BF16),
        pltpu.VMEM((2, 2, NX, BLOCK, WIDTH), BF16),
        pltpu.VMEM((2, NX, BLOCK, WIDTH), BF16),
        pltpu.VMEM((2, NX, BLOCK, WIDTH), BF16),
        pltpu.VMEM((2, NX - 1, BLOCK, WIDTH), BF16),
        pltpu.VMEM((2, NZ, OWN * CHUNKS, LANES), BF16),
        pltpu.VMEM((2, NZ - 1, OWN * CHUNKS, LANES), BF16),
        pltpu.VMEM((WIDTH, HID), BF16),
        pltpu.VMEM((WIDTH, HID), BF16),
        pltpu.VMEM((HID, WIDTH), BF16),
        dma((3,)),
        dma((3,)),
    ]
    for shape in (
        (2, NZ - 1), (2, NX - 1), (2, NX), (2, NY - 1), (2, NY - 1), (2, 2),
        (2, NY - 1), (2, NY - 1), (2,), (2, NX - 1), (2, NZ - 1),
    ):
        scratch += [dma(shape), dma(shape)]
    return pl.pallas_call(
        kernel,
        out_shape=(small, small, tall, tall, jax.ShapeDtypeStruct((HID, WIDTH), BF16)),
        in_specs=[vmem, vmem, hbm, hbm, hbm],
        out_specs=(vmem, vmem, hbm, hbm, hbm),
        scratch_shapes=scratch,
        compiler_params=pltpu.CompilerParams(
            collective_id=0, has_side_effects=True, vmem_limit_bytes=44 << 20
        ),
    )(activations, output_cotangent, gate_weight, up_weight, down_weight)


def solution(mesh):
    in_specs = (
        P(("dp", "col"), "row"),
        P("row", ("dp", "col")),
        P("row", ("dp", "col")),
        P(("dp", "col"), "row"),
        P(("dp", "col"), "row"),
    )
    out_specs = (
        P(("dp", "col"), "row"),
        P(("dp", "col"), "row"),
        P("row", ("dp", "col")),
        P("row", ("dp", "col")),
        P(("dp", "col"), "row"),
    )
    return jax.shard_map(body, mesh=mesh, in_specs=in_specs, out_specs=out_specs, check_vma=False)
```

```python
import jax
import jax.numpy as jnp
from jax import lax
from jax.experimental import pallas as pl
from jax.experimental.pallas import tpu as pltpu
from jax.sharding import PartitionSpec as P

MESH = pl.DeviceIdType.MESH
F32 = jnp.float32
BF16 = jnp.bfloat16
LANES = 128
OWN = 6
NX, NY, NZ = 4, 4, 8
BLOCK = OWN * NZ
HALF = NX * BLOCK
WIDTH = 1024
HID = 384
CHUNKS = WIDTH // LANES


def dot(left, right, dims):
    return lax.dot_general(left, right, (dims, ((), ())), preferred_element_type=F32)


def over_tokens(left, right):
    left, right = (v.reshape(2 * HALF, v.shape[-1]) for v in (left, right))
    return dot(left, right, ((0,), (0,))).astype(BF16)


def kernel(
    act_hbm, cot_hbm, gw_hbm, uw_hbm, dw_hbm,
    out_hbm, inp_hbm, gg_hbm, ug_hbm, dg_hbm,
    mine, wgu, wd, acts_t, zpiece, xall,
    gpart, grecv, gsend, gz, spart, srecv, ssend, sz, sums,
    hid, slope, part, crecv, xsend, xrecv, zsend, zrecv, rows_out, gradg, gradu, gradd, wsem, osem,
    z_s, z_r, x_s, x_r, c_s, c_r, yg_s, yg_r, ys_s, ys_r, e_s, e_r,
    yh_s, yh_r, yl_s, yl_r, fc_s, fc_r, fx_s, fx_r, fz_s, fz_r,
):
    dp, row, zl = lax.axis_index("dp"), lax.axis_index("row"), lax.axis_index("col")
    x, c = dp // 2, lax.rem(dp, 2)
    y, zh = row // 2, lax.rem(row, 2)

    sib = {"dp": x * 2 + 1 - c}
    far = {"row": y * 2 + 1 - zh}

    def xpos(i):
        return lax.rem(x + i, NX)

    def ypos(i):
        return lax.rem(y + i, NY)

    def zpos(i):
        return lax.rem(zl + i, NZ)

    def xdev(i):
        return {"dp": xpos(i) * 2 + c}

    def ydev(i):
        return {"row": ypos(i) * 2 + zh}

    def zdev(i):
        return {"col": zpos(i)}

    loads = [
        pltpu.make_async_copy(act_hbm, mine.at[0], wsem.at[3]),
        pltpu.make_async_copy(cot_hbm, mine.at[1], wsem.at[4]),
        pltpu.make_async_copy(gw_hbm, wgu.at[:, 0:HID], wsem.at[0]),
        pltpu.make_async_copy(uw_hbm, wgu.at[:, HID : 2 * HID], wsem.at[1]),
        pltpu.make_async_copy(dw_hbm, wd, wsem.at[2]),
    ]
    for load in loads:
        load.start()

    barrier = pltpu.get_barrier_semaphore()
    peers = [sib, far]
    peers += [xdev(i) for i in range(1, NX)]
    peers += [ydev(i) for i in range(1, NY)]
    peers += [zdev(i) for i in range(1, NZ)]
    for peer in peers:
        pl.semaphore_signal(barrier, inc=1, device_id=peer, device_id_type=MESH)

    def to_fine(value):
        return value.reshape(value.shape[0] * CHUNKS, LANES)

    def from_fine(value):
        return value.reshape(value.shape[0] // CHUNKS, WIDTH)

    for kind in range(2):
        loads[kind].wait()
        zpiece[kind, zl] = to_fine(mine[kind].astype(F32)).astype(BF16)

    pl.semaphore_wait(barrier, len(peers))

    started = []

    def send(src, dst, s, r, device):
        copy = pltpu.make_async_remote_copy(
            src_ref=src, dst_ref=dst, send_sem=s, recv_sem=r, device_id=device, device_id_type=MESH
        )
        copy.start()
        started.append(copy)
        return copy

    def z_gather(kind):
        return [
            send(zpiece.at[kind, zl], zpiece.at[kind, zl], z_s.at[kind, i], z_r.at[kind, i], zdev(i + 1))
            for i in range(NZ - 1)
        ]

    def forward(kind, where, i):
        block = xall.at[kind, c, where]
        return send(block, block, c_s.at[kind, i], c_r.at[kind, i], sib)

    def x_gather(kind, copies):
        for copy in copies:
            copy.wait_recv()
        pieces = zpiece[kind].reshape(NZ * OWN * CHUNKS, LANES).astype(F32)
        xall[kind, c, x] = from_fine(pieces).astype(BF16)
        block = xall.at[kind, c, x]
        xs = [
            send(block, block, x_s.at[kind, i], x_r.at[kind, i], xdev(i + 1))
            for i in range(NX - 1)
        ]
        return xs, [forward(kind, x, 0)]

    def pass_on(kind, xs, cs):
        for i in (0, 2, 1):
            xs[i].wait_recv()
            cs.append(forward(kind, lax.rem(x + NX - i - 1, NX), i + 1))

    def y_scatter(t, parts, recv, s, r):
        return [
            send(parts.at[t, ypos(i + 1)], recv.at[t, i], s.at[t, i], r.at[t, i], ydev(i + 1))
            for i in range(NY - 1)
        ]

    def y_gather(t, buf, s, r):
        return [
            send(buf.at[t, y], buf.at[t, y], s.at[t, i], r.at[t, i], ydev(i + 1))
            for i in range(NY - 1)
        ]

    def y_sum(t, copies, parts, recv, out):
        total = parts[t, y].astype(F32)
        for i in (0, 2, 1):
            copies[i].wait_recv()
            total = total + recv[t, i].astype(F32)
        out[t] = total.astype(BF16)

    stores = []

    def write(i, src, dst):
        stores.append(pltpu.make_async_copy(src, dst, osem.at[i]))
        stores[-1].start()

    def received(copies):
        for copy in copies:
            copy.wait_recv()

    def core_copy(k):
        return pltpu.make_async_remote_copy(
            src_ref=part.at[k, 1 - c], dst_ref=crecv.at[k], send_sem=fc_s.at[k],
            recv_sem=fc_r.at[k], device_id=sib, device_id_type=MESH,
        )

    def x_copy(k, i):
        return pltpu.make_async_remote_copy(
            src_ref=xsend.at[k, xpos(i + 1)], dst_ref=xrecv.at[k, i], send_sem=fx_s.at[k, i],
            recv_sem=fx_r.at[k, i], device_id=xdev(i + 1), device_id_type=MESH,
        )

    def scatter_core(k, t):
        @pl.when(c == 1 - t)
        def _():
            core_copy(k).start()

    def scatter_x(k, t):
        @pl.when(c == t)
        def _():
            core_copy(k).wait_recv()
            xsend[k] = (part[k, c].astype(F32) + crecv[k].astype(F32)).astype(BF16)
            for i in range(NX - 1):
                x_copy(k, i).start()

    def scatter_z(k):
        total = xsend[k, x].astype(F32)
        for i in (0, 2, 1):
            x_copy(k, i).wait_recv()
            total = total + xrecv[k, i].astype(F32)
        zsend[k] = to_fine(total).astype(BF16).reshape(NZ, OWN * CHUNKS, LANES)
        return [
            send(zsend.at[k, zpos(i + 1)], zrecv.at[k, i], fz_s.at[k, i], fz_r.at[k, i], zdev(i + 1))
            for i in range(NZ - 1)
        ]

    def finish(k, copies):
        total = zsend[k, zl].astype(F32)
        for i in range(NZ - 1):
            copies[i].wait_recv()
            total = total + zrecv[k, i].astype(F32)
        rows_out[k] = from_fine(total).astype(BF16)
        write(k, rows_out.at[k], (out_hbm, inp_hbm)[k])

    def exchange(t, k, src, dst):
        return send(src.at[t], dst.at[t], e_s.at[k, t], e_r.at[k, t], far)

    def block_terms(kind, t, weight, dims, parts):
        terms = dot(xall[kind, t].reshape(HALF, WIDTH), weight[...], dims)
        parts[t] = terms.astype(BF16).reshape(NY, BLOCK, terms.shape[-1])

    def hidden_units(t):
        both = gsend[t].astype(F32) + gz[t].astype(F32)
        sums[t] = both
        gate, up = both[:, 0:HID], both[:, HID : 2 * HID]
        hid[t, y] = (gate * jax.nn.sigmoid(gate) * up).astype(BF16)
        return y_gather(t, hid, yh_s, yh_r)

    def slope_pair(t):
        both = sums[t]
        gate, up = both[:, 0:HID], both[:, HID : 2 * HID]
        ds = ssend[t].astype(F32) + sz[t].astype(F32)
        s = jax.nn.sigmoid(gate)
        slope[t, y, :, 0:HID] = (ds * up * s * (1.0 + gate * (1.0 - s))).astype(BF16)
        slope[t, y, :, HID : 2 * HID] = (ds * gate * s).astype(BF16)
        return y_gather(t, slope, yl_s, yl_r)

    def outputs(t):
        total = dot(hid[t].reshape(HALF, HID), wd[...], ((1,), (0,)))
        part[0, t] = total.astype(BF16).reshape(NX, BLOCK, WIDTH)

    def input_slopes(t):
        total = dot(slope[t].reshape(HALF, 2 * HID), wgu[...], ((1,), (1,)))
        part[1, t] = total.astype(BF16).reshape(NX, BLOCK, WIDTH)

    az = z_gather(0)
    ax, ac = x_gather(0, az)
    cz = z_gather(1)
    pass_on(0, ax, ac)
    cx, cc = x_gather(1, cz)
    received(ac)
    loads[2].wait()
    loads[3].wait()

    yg, ys, eg, es = [], [], [], []
    for t in range(2):
        block_terms(0, t, wgu, ((1,), (0,)), gpart)
        yg.append(y_scatter(t, gpart, grecv, yg_s, yg_r))
    pass_on(1, cx, cc)
    y_sum(0, yg[0], gpart, grecv, gsend)
    eg.append(exchange(0, 0, gsend, gz))
    loads[4].wait()
    received(cc)
    for t in range(2):
        block_terms(1, t, wd, ((1,), (1,)), spart)
        ys.append(y_scatter(t, spart, srecv, ys_s, ys_r))
    y_sum(1, yg[1], gpart, grecv, gsend)
    eg.append(exchange(1, 0, gsend, gz))
    for t in range(2):
        y_sum(t, ys[t], spart, srecv, ssend)
        es.append(exchange(t, 1, ssend, sz))

    @pl.loop(0, CHUNKS)
    def _(j):
        at = pl.ds(pl.multiple_of(j * LANES, LANES), LANES)
        acts_t[at, :] = xall[0, :, :, :, at].reshape(2 * HALF, LANES).T

    received(eg[0:1])
    yh = [hidden_units(0)]
    received(yh[0])
    outputs(0)
    scatter_core(0, 0)
    received(eg[1:2])
    yh.append(hidden_units(1))
    scatter_x(0, 0)
    received(es[0:1])
    yl = [slope_pair(0)]
    received(yh[1])
    outputs(1)
    scatter_core(0, 1)
    scatter_x(0, 1)
    @pl.loop(0, HID // LANES)
    def _(j):
        at = pl.ds(pl.multiple_of(j * LANES, LANES), LANES)
        gradd[at, :] = over_tokens(hid[:, :, :, at], xall[1])

    write(4, gradd, dg_hbm)
    received(es[1:2])
    yl.append(slope_pair(1))
    received(yl[0])
    input_slopes(0)
    scatter_core(1, 0)
    fz_o = scatter_z(0)
    scatter_x(1, 0)
    received(yl[1])
    input_slopes(1)
    scatter_core(1, 1)
    scatter_x(1, 1)
    @pl.loop(0, CHUNKS // 2)
    def _(j):
        at = pl.ds(pl.multiple_of(j * 2 * LANES, 2 * LANES), 2 * LANES)
        grads = dot(acts_t[at, :], slope[...].reshape(2 * HALF, 2 * HID), ((1,), (0,)))
        gradg[at, :] = grads[:, 0:HID].astype(BF16)
        gradu[at, :] = grads[:, HID : 2 * HID].astype(BF16)

    write(2, gradg, gg_hbm)
    write(3, gradu, ug_hbm)
    finish(0, fz_o)
    fz_i = scatter_z(1)
    finish(1, fz_i)
    for k in range(2):
        core_copy(k).wait_send()
        for i in range(NX - 1):
            x_copy(k, i).wait_send()
    for copy in started:
        copy.wait_send()
    for copy in stores:
        copy.wait()


def store(*refs):
    given, results, held = refs[0:5], refs[5:10], refs[10:15]
    sems = refs[15]
    copies = []
    for i in range(5):
        copies.append(
            (
                pltpu.make_async_copy(given[i], held[i], sems.at[0, i]),
                pltpu.make_async_copy(held[i], results[i], sems.at[1, i]),
            )
        )
        copies[i][0].start()
    for read, write in copies:
        read.wait()
        write.start()
    for _, write in copies:
        write.wait()


def body(activations, gate_weight, up_weight, down_weight, output_cotangent):
    hbm = pl.BlockSpec(memory_space=pltpu.HBM)
    dma = pltpu.SemaphoreType.DMA
    small = jax.ShapeDtypeStruct((OWN, WIDTH), BF16)
    tall = jax.ShapeDtypeStruct((WIDTH, HID), BF16)
    scratch = [
        pltpu.VMEM((2, OWN, WIDTH), BF16),
        pltpu.VMEM((WIDTH, 2 * HID), BF16),
        pltpu.VMEM((HID, WIDTH), BF16),
        pltpu.VMEM((WIDTH, 2 * HALF), BF16),
        pltpu.VMEM((2, NZ, OWN * CHUNKS, LANES), BF16),
        pltpu.VMEM((2, 2, NX, BLOCK, WIDTH), BF16),
        pltpu.VMEM((2, NY, BLOCK, 2 * HID), BF16),
        pltpu.VMEM((2, NY - 1, BLOCK, 2 * HID), BF16),
        pltpu.VMEM((2, BLOCK, 2 * HID), BF16),
        pltpu.VMEM((2, BLOCK, 2 * HID), BF16),
        pltpu.VMEM((2, NY, BLOCK, HID), BF16),
        pltpu.VMEM((2, NY - 1, BLOCK, HID), BF16),
        pltpu.VMEM((2, BLOCK, HID), BF16),
        pltpu.VMEM((2, BLOCK, HID), BF16),
        pltpu.VMEM((2, BLOCK, 2 * HID), F32),
        pltpu.VMEM((2, NY, BLOCK, HID), BF16),
        pltpu.VMEM((2, NY, BLOCK, 2 * HID), BF16),
        pltpu.VMEM((2, 2, NX, BLOCK, WIDTH), BF16),
        pltpu.VMEM((2, NX, BLOCK, WIDTH), BF16),
        pltpu.VMEM((2, NX, BLOCK, WIDTH), BF16),
        pltpu.VMEM((2, NX - 1, BLOCK, WIDTH), BF16),
        pltpu.VMEM((2, NZ, OWN * CHUNKS, LANES), BF16),
        pltpu.VMEM((2, NZ - 1, OWN * CHUNKS, LANES), BF16),
        pltpu.VMEM((2, OWN, WIDTH), BF16),
        pltpu.VMEM((WIDTH, HID), BF16),
        pltpu.VMEM((WIDTH, HID), BF16),
        pltpu.VMEM((HID, WIDTH), BF16),
        dma((5,)),
        dma((5,)),
    ]
    for shape in (
        (2, NZ - 1), (2, NX - 1), (2, NX), (2, NY - 1), (2, NY - 1), (2, 2),
        (2, NY - 1), (2, NY - 1), (2,), (2, NX - 1), (2, NZ - 1),
    ):
        scratch += [dma(shape), dma(shape)]
    shapes = (small, small, tall, tall, jax.ShapeDtypeStruct((HID, WIDTH), BF16))
    results = pl.pallas_call(
        kernel,
        out_shape=shapes,
        in_specs=[hbm] * 5,
        out_specs=(hbm,) * 5,
        scratch_shapes=scratch,
        compiler_params=pltpu.CompilerParams(
            collective_id=0, has_side_effects=True, vmem_limit_bytes=61 << 20
        ),
    )(activations, output_cotangent, gate_weight, up_weight, down_weight)
    return pl.pallas_call(
        store,
        out_shape=shapes,
        in_specs=[hbm] * 5,
        out_specs=(hbm,) * 5,
        scratch_shapes=[pltpu.VMEM(s.shape, s.dtype) for s in shapes] + [dma((2, 5))],
    )(*results)


def solution(mesh):
    in_specs = (
        P(("dp", "col"), "row"),
        P("row", ("dp", "col")),
        P("row", ("dp", "col")),
        P(("dp", "col"), "row"),
        P(("dp", "col"), "row"),
    )
    out_specs = (
        P(("dp", "col"), "row"),
        P(("dp", "col"), "row"),
        P("row", ("dp", "col")),
        P("row", ("dp", "col")),
        P(("dp", "col"), "row"),
    )
    return jax.shard_map(body, mesh=mesh, in_specs=in_specs, out_specs=out_specs, check_vma=False)
```

```python
import jax
import jax.numpy as jnp
from jax import lax
from jax.experimental import pallas as pl
from jax.experimental.pallas import tpu as pltpu
from jax.sharding import PartitionSpec as P

MESH = pl.DeviceIdType.MESH
F32 = jnp.float32
BF16 = jnp.bfloat16
LANES = 128
OWN = 6
NX, NY, NZ = 4, 4, 8
BLOCK = OWN * NZ
HALF = NX * BLOCK
WIDTH = 1024
HID = 384
CHUNKS = WIDTH // LANES


def dot(left, right, dims):
    return lax.dot_general(left, right, (dims, ((), ())), preferred_element_type=F32)


def over_tokens(left, right):
    left, right = (v.reshape(2 * HALF, v.shape[-1]) for v in (left, right))
    return dot(left, right, ((0,), (0,))).astype(BF16)


def kernel(
    act_hbm, cot_hbm, gw_hbm, uw_hbm, dw_hbm,
    out_hbm, inp_hbm, gg_hbm, ug_hbm, dg_hbm,
    mine, wgu, wd, acts_t, xfine, xall, terms, trecv, tsend, tfar, sums,
    hid, slope, part, crecv, xsend, xrecv, zsend, zrecv, rows_out, gradg, gradu, gradd, wsem, osem,
    z_s, z_r, x_s, x_r, c_s, c_r, y_s, y_r, e_s, e_r,
    yh_s, yh_r, yl_s, yl_r, fc_s, fc_r, fx_s, fx_r, fz_s, fz_r,
):
    dp, row, zl = lax.axis_index("dp"), lax.axis_index("row"), lax.axis_index("col")
    x, c = dp // 2, lax.rem(dp, 2)
    y, zh = row // 2, lax.rem(row, 2)

    sib = {"dp": x * 2 + 1 - c}
    far = {"row": y * 2 + 1 - zh}

    half = zl // 4

    def xpos(i):
        return lax.rem(x + i, NX)

    def ypos(i):
        return lax.rem(y + i, NY)

    def zpos(m):
        place = 0
        for bit in (4, 2, 1):
            mine_ = lax.rem(zl // bit, 2)
            place = place + bit * (1 - mine_ if m & bit else mine_)
        return place

    def fours(order):
        return pl.ds(4 * (half if order == 0 else 1 - half), 4)

    def xdev(i):
        return {"dp": xpos(i) * 2 + c}

    def ydev(i):
        return {"row": ypos(i) * 2 + zh}

    def zdev(m):
        return {"col": zpos(m)}

    loads = [
        pltpu.make_async_copy(act_hbm, mine.at[0], wsem.at[3]),
        pltpu.make_async_copy(cot_hbm, mine.at[1], wsem.at[4]),
        pltpu.make_async_copy(gw_hbm, wgu.at[:, 0:HID], wsem.at[0]),
        pltpu.make_async_copy(uw_hbm, wgu.at[:, HID : 2 * HID], wsem.at[1]),
        pltpu.make_async_copy(dw_hbm, wd, wsem.at[2]),
    ]
    for load in loads:
        load.start()

    barrier = pltpu.get_barrier_semaphore()
    peers = [sib, far]
    peers += [xdev(i) for i in range(1, NX)]
    peers += [ydev(i) for i in range(1, NY)]
    peers += [zdev(m) for m in range(1, NZ)]
    for peer in peers:
        pl.semaphore_signal(barrier, inc=1, device_id=peer, device_id_type=MESH)

    def to_fine(value):
        return value.reshape(value.shape[0] * CHUNKS, LANES)

    def from_fine(value):
        return value.reshape(value.shape[0] // CHUNKS, WIDTH)

    for kind in range(2):
        loads[kind].wait()
        xfine[kind, c, x, zl] = to_fine(mine[kind].astype(F32)).astype(BF16)

    pl.semaphore_wait(barrier, len(peers))

    started = []

    def send(src, dst, s, r, device):
        copy = pltpu.make_async_remote_copy(
            src_ref=src, dst_ref=dst, send_sem=s, recv_sem=r, device_id=device, device_id_type=MESH
        )
        copy.start()
        started.append(copy)
        return copy

    def z_gather(kind):
        piece = xfine.at[kind, c, x, zl]
        copies = {}
        for m in (7, 6, 5, 4, 3, 2, 1):
            copies[m] = send(piece, piece, z_s.at[kind, m - 1], z_r.at[kind, m - 1], zdev(m))
        return copies

    def forward(kind, where, order, i):
        block = xfine.at[kind, c, where, fours(order)]
        return send(block, block, c_s.at[kind, order, i], c_r.at[kind, order, i], sib)

    def x_gather(kind, copies):
        xs, cs = [], []
        for order in range(2):
            for m in ((1, 2, 3), (4, 5, 6, 7))[order]:
                copies[m].wait_recv()
            block = xfine.at[kind, c, x, fours(order)]
            for i in range(NX - 1):
                sems = x_s.at[kind, order, i], x_r.at[kind, order, i]
                xs.append(send(block, block, *sems, xdev(i + 1)))
            cs.append(forward(kind, x, order, 0))
        return xs, cs

    def pass_on(kind, xs, cs):
        for order in range(2):
            for i in (0, 2, 1):
                xs[order * (NX - 1) + i].wait_recv()
                cs.append(forward(kind, lax.rem(x + NX - i - 1, NX), order, i + 1))

    def lay_out(kind, t):
        for where in range(NX):
            pieces = xfine[kind, t, where].reshape(BLOCK * CHUNKS, LANES)
            xall[kind, t, where] = from_fine(pieces.astype(F32)).astype(BF16)

    def y_scatter(q, k):
        return [
            send(
                terms.at[q, k, ypos(i + 1)], trecv.at[q, k, i],
                y_s.at[q, k, i], y_r.at[q, k, i], ydev(i + 1),
            )
            for i in range(NY - 1)
        ]

    def y_sum(q, k, copies):
        total = terms[q, k, y].astype(F32)
        for i in (0, 2, 1):
            copies[i].wait_recv()
            total = total + trecv[q, k, i].astype(F32)
        tsend[q, k] = total.astype(BF16)
        return send(tsend.at[q, k], tfar.at[q, k], e_s.at[q, k], e_r.at[q, k], far)

    def whole(q, k):
        return tsend[q, k].astype(F32) + tfar[q, k].astype(F32)

    def y_gather(t, k, buf, s, r):
        return [
            send(buf.at[t, y], buf.at[t, y], s.at[k, i], r.at[k, i], ydev(i + 1))
            for i in range(NY - 1)
        ]

    stores = []

    def write(i, src, dst):
        stores.append(pltpu.make_async_copy(src, dst, osem.at[i]))
        stores[-1].start()

    def received(copies):
        for copy in copies:
            copy.wait_recv()

    def core_copy(k):
        return pltpu.make_async_remote_copy(
            src_ref=part.at[k, 1 - c], dst_ref=crecv.at[k], send_sem=fc_s.at[k],
            recv_sem=fc_r.at[k], device_id=sib, device_id_type=MESH,
        )

    def x_copy(k, order, i):
        at = fours(1 - order)
        return pltpu.make_async_remote_copy(
            src_ref=xsend.at[k, xpos(i + 1), at], dst_ref=xrecv.at[k, i, at],
            send_sem=fx_s.at[k, order, i], recv_sem=fx_r.at[k, order, i],
            device_id=xdev(i + 1), device_id_type=MESH,
        )

    def scatter_core(k, t):
        @pl.when(c == 1 - t)
        def _():
            core_copy(k).start()

    def scatter_x(k, t):
        @pl.when(c == t)
        def _():
            core_copy(k).wait_recv()
            for where in range(NX):
                total = part[k, c, where].astype(F32) + crecv[k, where].astype(F32)
                xsend[k, where] = to_fine(total).astype(BF16).reshape(NZ, OWN * CHUNKS, LANES)
            for order in range(2):
                for i in range(NX - 1):
                    x_copy(k, order, i).start()

    def scatter_z(k):
        copies = []
        for order in range(2):
            at = fours(1 - order)
            total = xsend[k, x, at].astype(F32)
            for i in (0, 2, 1):
                x_copy(k, order, i).wait_recv()
                total = total + xrecv[k, i, at].astype(F32)
            zsend[k, at] = total.astype(BF16)
            for m in ((7, 6, 5, 4), (3, 2, 1))[order]:
                sems = fz_s.at[k, m - 1], fz_r.at[k, m - 1]
                copies.append(send(zsend.at[k, zpos(m)], zrecv.at[k, m - 1], *sems, zdev(m)))
        return copies

    def finish(k, copies):
        total = zsend[k, zl].astype(F32)
        received(copies)
        for i in range(NZ - 1):
            total = total + zrecv[k, i].astype(F32)
        rows_out[k] = from_fine(total).astype(BF16)
        write(k, rows_out.at[k], (out_hbm, inp_hbm)[k])

    def gate_up_terms(t, k):
        both = dot(xall[0, t].reshape(HALF, WIDTH), wgu[...], ((1,), (0,))).astype(BF16)
        copies = []
        for q in range(2):
            terms[q, k] = both[:, q * HID : (q + 1) * HID].reshape(NY, BLOCK, HID)
            copies.append(y_scatter(q, k))
        return copies

    def slope_terms(t):
        terms[2, t] = (
            dot(xall[1, t].reshape(HALF, WIDTH), wd[...], ((1,), (1,)))
            .astype(BF16)
            .reshape(NY, BLOCK, HID)
        )
        return y_scatter(2, t)

    def hidden_units(t, k):
        gate, up = whole(0, k), whole(1, k)
        sums[0, t], sums[1, t] = gate, up
        hid[t, y] = (gate * jax.nn.sigmoid(gate) * up).astype(BF16)
        return y_gather(t, k, hid, yh_s, yh_r)

    def slope_pair(t):
        gate, up, ds = sums[0, t], sums[1, t], whole(2, t)
        s = jax.nn.sigmoid(gate)
        slope[t, y, :, 0:HID] = (ds * up * s * (1.0 + gate * (1.0 - s))).astype(BF16)
        slope[t, y, :, HID : 2 * HID] = (ds * gate * s).astype(BF16)
        return y_gather(t, t, slope, yl_s, yl_r)

    def outputs(t):
        total = dot(hid[t].reshape(HALF, HID), wd[...], ((1,), (0,)))
        part[0, t] = total.astype(BF16).reshape(NX, BLOCK, WIDTH)

    def input_slopes(t):
        total = dot(slope[t].reshape(HALF, 2 * HID), wgu[...], ((1,), (1,)))
        part[1, t] = total.astype(BF16).reshape(NX, BLOCK, WIDTH)

    az = z_gather(0)
    ax, ac = x_gather(0, az)
    cz = z_gather(1)
    pass_on(0, ax, ac)
    lay_out(0, c)
    loads[2].wait()
    loads[3].wait()
    yg = [gate_up_terms(c, 0)]
    received(ac)
    lay_out(0, 1 - c)
    yg.append(gate_up_terms(1 - c, 1))
    cx, cc = x_gather(1, cz)
    eg = [y_sum(0, 0, yg[0][0]), y_sum(1, 0, yg[0][1])]
    pass_on(1, cx, cc)
    loads[4].wait()
    eg.append(y_sum(0, 1, yg[1][0]))
    received(cc)
    ys = []
    for t in range(2):
        lay_out(1, t)
        ys.append(slope_terms(t))
    eg.append(y_sum(1, 1, yg[1][1]))
    es = [y_sum(2, t, ys[t]) for t in range(2)]

    @pl.loop(0, CHUNKS)
    def _(j):
        at = pl.ds(pl.multiple_of(j * LANES, LANES), LANES)
        acts_t[at, :] = xall[0, :, :, :, at].reshape(2 * HALF, LANES).T

    received(eg[0:2])
    yh = hidden_units(c, 0)
    received(eg[2:4])
    yh += hidden_units(1 - c, 1)
    received(es[0:1])
    yl = [slope_pair(0)]
    received(yh)
    for t in range(2):
        outputs(t)
        scatter_core(0, t)
    for t in range(2):
        scatter_x(0, t)
    received(es[1:2])
    yl.append(slope_pair(1))

    @pl.loop(0, HID // LANES)
    def _(j):
        at = pl.ds(pl.multiple_of(j * LANES, LANES), LANES)
        gradd[at, :] = over_tokens(hid[:, :, :, at], xall[1])

    write(4, gradd, dg_hbm)
    received(yl[0])
    input_slopes(0)
    scatter_core(1, 0)
    scatter_x(1, 0)
    fz_o = scatter_z(0)
    received(yl[1])
    input_slopes(1)
    scatter_core(1, 1)
    scatter_x(1, 1)

    @pl.loop(0, CHUNKS // 2)
    def _(j):
        at = pl.ds(pl.multiple_of(j * 2 * LANES, 2 * LANES), 2 * LANES)
        grads = dot(acts_t[at, :], slope[...].reshape(2 * HALF, 2 * HID), ((1,), (0,)))
        gradg[at, :] = grads[:, 0:HID].astype(BF16)
        gradu[at, :] = grads[:, HID : 2 * HID].astype(BF16)

    write(2, gradg, gg_hbm)
    write(3, gradu, ug_hbm)
    fz_i = scatter_z(1)
    finish(0, fz_o)
    finish(1, fz_i)
    for k in range(2):
        core_copy(k).wait_send()
        for order in range(2):
            for i in range(NX - 1):
                x_copy(k, order, i).wait_send()
    for copy in started:
        copy.wait_send()
    for copy in stores:
        copy.wait()


def store(*refs):
    given, results, held = refs[0:5], refs[5:10], refs[10:15]
    sems = refs[15]
    copies = []
    for i in range(5):
        copies.append(
            (
                pltpu.make_async_copy(given[i], held[i], sems.at[0, i]),
                pltpu.make_async_copy(held[i], results[i], sems.at[1, i]),
            )
        )
        copies[i][0].start()
    for read, write in copies:
        read.wait()
        write.start()
    for _, write in copies:
        write.wait()


def body(activations, gate_weight, up_weight, down_weight, output_cotangent):
    hbm = pl.BlockSpec(memory_space=pltpu.HBM)
    dma = pltpu.SemaphoreType.DMA
    small = jax.ShapeDtypeStruct((OWN, WIDTH), BF16)
    tall = jax.ShapeDtypeStruct((WIDTH, HID), BF16)
    scratch = [
        pltpu.VMEM((2, OWN, WIDTH), BF16),
        pltpu.VMEM((WIDTH, 2 * HID), BF16),
        pltpu.VMEM((HID, WIDTH), BF16),
        pltpu.VMEM((WIDTH, 2 * HALF), BF16),
        pltpu.VMEM((2, 2, NX, NZ, OWN * CHUNKS, LANES), BF16),
        pltpu.VMEM((2, 2, NX, BLOCK, WIDTH), BF16),
        pltpu.VMEM((3, 2, NY, BLOCK, HID), BF16),
        pltpu.VMEM((3, 2, NY - 1, BLOCK, HID), BF16),
        pltpu.VMEM((3, 2, BLOCK, HID), BF16),
        pltpu.VMEM((3, 2, BLOCK, HID), BF16),
        pltpu.VMEM((2, 2, BLOCK, HID), F32),
        pltpu.VMEM((2, NY, BLOCK, HID), BF16),
        pltpu.VMEM((2, NY, BLOCK, 2 * HID), BF16),
        pltpu.VMEM((2, 2, NX, BLOCK, WIDTH), BF16),
        pltpu.VMEM((2, NX, BLOCK, WIDTH), BF16),
        pltpu.VMEM((2, NX, NZ, OWN * CHUNKS, LANES), BF16),
        pltpu.VMEM((2, NX - 1, NZ, OWN * CHUNKS, LANES), BF16),
        pltpu.VMEM((2, NZ, OWN * CHUNKS, LANES), BF16),
        pltpu.VMEM((2, NZ - 1, OWN * CHUNKS, LANES), BF16),
        pltpu.VMEM((2, OWN, WIDTH), BF16),
        pltpu.VMEM((WIDTH, HID), BF16),
        pltpu.VMEM((WIDTH, HID), BF16),
        pltpu.VMEM((HID, WIDTH), BF16),
        dma((5,)),
        dma((5,)),
    ]
    for shape in (
        (2, NZ - 1), (2, 2, NX - 1), (2, 2, NX), (3, 2, NY - 1), (3, 2),
        (2, NY - 1), (2, NY - 1), (2,), (2, 2, NX - 1), (2, NZ - 1),
    ):
        scratch += [dma(shape), dma(shape)]
    shapes = (small, small, tall, tall, jax.ShapeDtypeStruct((HID, WIDTH), BF16))
    results = pl.pallas_call(
        kernel,
        out_shape=shapes,
        in_specs=[hbm] * 5,
        out_specs=(hbm,) * 5,
        scratch_shapes=scratch,
        compiler_params=pltpu.CompilerParams(
            collective_id=0, has_side_effects=True, vmem_limit_bytes=61 << 20
        ),
    )(activations, output_cotangent, gate_weight, up_weight, down_weight)
    return pl.pallas_call(
        store,
        out_shape=shapes,
        in_specs=[hbm] * 5,
        out_specs=(hbm,) * 5,
        scratch_shapes=[pltpu.VMEM(s.shape, s.dtype) for s in shapes] + [dma((2, 5))],
    )(*results)


def solution(mesh):
    in_specs = (
        P(("dp", "col"), "row"),
        P("row", ("dp", "col")),
        P("row", ("dp", "col")),
        P(("dp", "col"), "row"),
        P(("dp", "col"), "row"),
    )
    out_specs = (
        P(("dp", "col"), "row"),
        P(("dp", "col"), "row"),
        P("row", ("dp", "col")),
        P("row", ("dp", "col")),
        P(("dp", "col"), "row"),
    )
    return jax.shard_map(body, mesh=mesh, in_specs=in_specs, out_specs=out_specs, check_vma=False)
```

```python
import jax
import jax.numpy as jnp
from jax import lax
from jax.experimental import pallas as pl
from jax.experimental.pallas import tpu as pltpu
from jax.sharding import PartitionSpec as P

MESH = pl.DeviceIdType.MESH
F32 = jnp.float32
BF16 = jnp.bfloat16
LANES = 128
OWN = 6
NX, NY, NZ = 4, 4, 8
BLOCK = OWN * NZ
HALF = NX * BLOCK
WIDTH = 1024
HID = 384
CHUNKS = WIDTH // LANES


def dot(left, right, dims):
    return lax.dot_general(left, right, (dims, ((), ())), preferred_element_type=F32)


def over_tokens(left, right):
    left, right = (v.reshape(2 * HALF, v.shape[-1]) for v in (left, right))
    return dot(left, right, ((0,), (0,))).astype(BF16)


def kernel(
    act_hbm, cot_hbm, gw_hbm, uw_hbm, dw_hbm,
    out_hbm, inp_hbm, gg_hbm, ug_hbm, dg_hbm,
    mine, wgu, wd, acts_t, xfine, xall, terms, trecv, tsend, tfar, sums,
    hid, slope, part, crecv, xsend, xrecv, zsend, zrecv, rows_out, gradg, gradu, gradd, wsem, osem,
    z_s, z_r, x_s, x_r, c_s, c_r, y_s, y_r, e_s, e_r,
    yh_s, yh_r, yl_s, yl_r, fc_s, fc_r, fx_s, fx_r, fz_s, fz_r,
):
    dp, row, zl = lax.axis_index("dp"), lax.axis_index("row"), lax.axis_index("col")
    x, c = dp // 2, lax.rem(dp, 2)
    y, zh = row // 2, lax.rem(row, 2)

    sib = {"dp": x * 2 + 1 - c}
    far = {"row": y * 2 + 1 - zh}

    half = zl // 4

    def xpos(i):
        return lax.rem(x + i, NX)

    def ypos(i):
        return lax.rem(y + i, NY)

    def zpos(m):
        place = 0
        for bit in (4, 2, 1):
            mine_ = lax.rem(zl // bit, 2)
            place = place + bit * (1 - mine_ if m & bit else mine_)
        return place

    def fours(order):
        return pl.ds(4 * (half if order == 0 else 1 - half), 4)

    def xdev(i):
        return {"dp": xpos(i) * 2 + c}

    def ydev(i):
        return {"row": ypos(i) * 2 + zh}

    def zdev(m):
        return {"col": zpos(m)}

    barrier = pltpu.get_barrier_semaphore()
    peers = [far] + [zdev(m) for m in range(NZ - 1, 0, -1)]
    peers += [ydev(i) for i in range(1, NY)]
    peers += [xdev(i) for i in range(1, NX)] + [sib]
    for peer in peers:
        pl.semaphore_signal(barrier, inc=1, device_id=peer, device_id_type=MESH)

    loads = [
        pltpu.make_async_copy(act_hbm, mine.at[0], wsem.at[3]),
        pltpu.make_async_copy(cot_hbm, mine.at[1], wsem.at[4]),
        pltpu.make_async_copy(gw_hbm, wgu.at[:, 0:HID], wsem.at[0]),
        pltpu.make_async_copy(uw_hbm, wgu.at[:, HID : 2 * HID], wsem.at[1]),
        pltpu.make_async_copy(dw_hbm, wd, wsem.at[2]),
    ]
    for load in loads[0:2]:
        load.start()

    def to_fine(value):
        return value.reshape(value.shape[0] * CHUNKS, LANES)

    def from_fine(value):
        return value.reshape(value.shape[0] // CHUNKS, WIDTH)

    for kind in range(2):
        loads[kind].wait()
        xfine[kind, c, x, zl] = to_fine(mine[kind].astype(F32)).astype(BF16)

    pl.semaphore_wait(barrier, len(peers))

    started = []

    def send(src, dst, s, r, device):
        copy = pltpu.make_async_remote_copy(
            src_ref=src, dst_ref=dst, send_sem=s, recv_sem=r, device_id=device, device_id_type=MESH
        )
        copy.start()
        started.append(copy)
        return copy

    def z_gather(kind):
        piece = xfine.at[kind, c, x, zl]
        copies = {}
        for m in (1, 2, 3, 4, 5, 6, 7):
            copies[m] = send(piece, piece, z_s.at[kind, m - 1], z_r.at[kind, m - 1], zdev(m))
        return copies

    def forward(kind, where, order, i):
        block = xfine.at[kind, c, where, fours(order)]
        return send(block, block, c_s.at[kind, order, i], c_r.at[kind, order, i], sib)

    def x_gather(kind, copies):
        xs, cs = [], []
        for order in range(2):
            for m in ((1, 2, 3), (4, 5, 6, 7))[order]:
                copies[m].wait_recv()
            block = xfine.at[kind, c, x, fours(order)]
            for i in range(NX - 1):
                sems = x_s.at[kind, order, i], x_r.at[kind, order, i]
                xs.append(send(block, block, *sems, xdev(i + 1)))
            cs.append(forward(kind, x, order, 0))
        return xs, cs

    def lay_out(kind, t, where):
        pieces = xfine[kind, t, where].reshape(BLOCK * CHUNKS, LANES)
        xall[kind, t, where] = from_fine(pieces.astype(F32)).astype(BF16)

    def pass_on(kind, xs, cs):
        lay_out(kind, c, x)
        for order in range(2):
            for i in (0, 2, 1):
                where = lax.rem(x + NX - i - 1, NX)
                xs[order * (NX - 1) + i].wait_recv()
                cs.append(forward(kind, where, order, i + 1))
                if order == 1:
                    lay_out(kind, c, where)

    def from_sibling(kind, cs):
        received(cs)
        for where in range(NX):
            lay_out(kind, 1 - c, where)

    def y_scatter(q, k):
        return [
            send(
                terms.at[q, k, ypos(i + 1)], trecv.at[q, k, i],
                y_s.at[q, k, i], y_r.at[q, k, i], ydev(i + 1),
            )
            for i in range(NY - 1)
        ]

    def y_sum(q, k, copies):
        total = terms[q, k, y].astype(F32)
        for i in (0, 2, 1):
            copies[i].wait_recv()
            total = total + trecv[q, k, i].astype(F32)
        tsend[q, k] = total.astype(BF16)
        return send(tsend.at[q, k], tfar.at[q, k], e_s.at[q, k], e_r.at[q, k], far)

    def whole(q, k):
        return tsend[q, k].astype(F32) + tfar[q, k].astype(F32)

    def y_gather(t, k, buf, s, r):
        return [
            send(buf.at[t, y], buf.at[t, y], s.at[k, i], r.at[k, i], ydev(i + 1))
            for i in range(NY - 1)
        ]

    stores = []

    def write(i, src, dst):
        stores.append(pltpu.make_async_copy(src, dst, osem.at[i]))
        stores[-1].start()

    def received(copies):
        for copy in copies:
            copy.wait_recv()

    def core_copy(k, i):
        where = xpos(i)
        return pltpu.make_async_remote_copy(
            src_ref=part.at[k, 1 - c, where], dst_ref=crecv.at[k, where], send_sem=fc_s.at[k, i],
            recv_sem=fc_r.at[k, i], device_id=sib, device_id_type=MESH,
        )

    def x_copy(k, order, i):
        at = fours(1 - order)
        return pltpu.make_async_remote_copy(
            src_ref=xsend.at[k, xpos(i + 1), at], dst_ref=xrecv.at[k, i, at],
            send_sem=fx_s.at[k, order, i], recv_sem=fx_r.at[k, order, i],
            device_id=xdev(i + 1), device_id_type=MESH,
        )

    def scatter_core(k, t):
        @pl.when(c == 1 - t)
        def _():
            for i in (2, 1, 3, 0):
                core_copy(k, i).start()

    def scatter_x(k, t):
        @pl.when(c == t)
        def _():
            for i in (2, 1, 3, 0):
                where = xpos(i)
                core_copy(k, i).wait_recv()
                total = part[k, c, where].astype(F32) + crecv[k, where].astype(F32)
                xsend[k, where] = to_fine(total).astype(BF16).reshape(NZ, OWN * CHUNKS, LANES)
                if i > 0:
                    for order in range(2):
                        x_copy(k, order, i - 1).start()

    def scatter_z(k):
        copies = []
        for order in range(2):
            at = fours(1 - order)
            total = xsend[k, x, at].astype(F32)
            for i in (0, 2, 1):
                x_copy(k, order, i).wait_recv()
                total = total + xrecv[k, i, at].astype(F32)
            zsend[k, at] = total.astype(BF16)
            for m in ((7, 6, 5, 4), (3, 2, 1))[order]:
                sems = fz_s.at[k, m - 1], fz_r.at[k, m - 1]
                copies.append(send(zsend.at[k, zpos(m)], zrecv.at[k, m - 1], *sems, zdev(m)))
        return copies

    def finish(k, copies):
        total = zsend[k, zl].astype(F32)
        received(copies)
        for i in range(NZ - 1):
            total = total + zrecv[k, i].astype(F32)
        rows_out[k] = from_fine(total).astype(BF16)
        write(k, rows_out.at[k], (out_hbm, inp_hbm)[k])

    def gate_up_terms(t, k):
        both = dot(xall[0, t].reshape(HALF, WIDTH), wgu[...], ((1,), (0,))).astype(BF16)
        copies = []
        for q in range(2):
            terms[q, k] = both[:, q * HID : (q + 1) * HID].reshape(NY, BLOCK, HID)
            copies.append(y_scatter(q, k))
        return copies

    def slope_terms(t):
        terms[2, t] = (
            dot(xall[1, t].reshape(HALF, WIDTH), wd[...], ((1,), (1,)))
            .astype(BF16)
            .reshape(NY, BLOCK, HID)
        )
        return y_scatter(2, t)

    def hidden_units(t, k):
        gate, up = whole(0, k), whole(1, k)
        sums[0, t], sums[1, t] = gate, up
        hid[t, y] = (gate * jax.nn.sigmoid(gate) * up).astype(BF16)
        return y_gather(t, k, hid, yh_s, yh_r)

    def slope_pair(t):
        gate, up, ds = sums[0, t], sums[1, t], whole(2, t)
        s = jax.nn.sigmoid(gate)
        slope[t, y, :, 0:HID] = (ds * up * s * (1.0 + gate * (1.0 - s))).astype(BF16)
        slope[t, y, :, HID : 2 * HID] = (ds * gate * s).astype(BF16)
        return y_gather(t, t, slope, yl_s, yl_r)

    def outputs(t):
        total = dot(hid[t].reshape(HALF, HID), wd[...], ((1,), (0,)))
        part[0, t] = total.astype(BF16).reshape(NX, BLOCK, WIDTH)

    def input_slopes(t):
        total = dot(slope[t].reshape(HALF, 2 * HID), wgu[...], ((1,), (1,)))
        part[1, t] = total.astype(BF16).reshape(NX, BLOCK, WIDTH)

    az = z_gather(0)
    for load in loads[2:5]:
        load.start()
    ax, ac = x_gather(0, az)
    cz = z_gather(1)
    pass_on(0, ax, ac)
    loads[2].wait()
    loads[3].wait()
    yg = [gate_up_terms(c, 0)]
    from_sibling(0, ac)
    yg.append(gate_up_terms(1 - c, 1))
    cx, cc = x_gather(1, cz)
    eg = [y_sum(0, 0, yg[0][0]), y_sum(1, 0, yg[0][1])]
    pass_on(1, cx, cc)
    loads[4].wait()
    eg.append(y_sum(0, 1, yg[1][0]))
    from_sibling(1, cc)
    ys = [slope_terms(t) for t in range(2)]
    eg.append(y_sum(1, 1, yg[1][1]))
    gathers = [copy for copy in started if all(copy is not other for other in eg)]
    es = [y_sum(2, t, ys[t]) for t in range(2)]

    @pl.loop(0, CHUNKS)
    def _(j):
        at = pl.ds(pl.multiple_of(j * LANES, LANES), LANES)
        acts_t[at, :] = xall[0, :, :, :, at].reshape(2 * HALF, LANES).T

    for copy in gathers:
        copy.wait_send()

    received(eg[0:2])
    yh = hidden_units(c, 0)
    received(eg[2:4])
    yh += hidden_units(1 - c, 1)
    received(es[0:1])
    yl = [slope_pair(0)]
    received(yh)
    for t in range(2):
        outputs(t)
        scatter_core(0, t)
    for t in range(2):
        scatter_x(0, t)
    received(es[1:2])
    yl.append(slope_pair(1))

    @pl.loop(0, HID // LANES)
    def _(j):
        at = pl.ds(pl.multiple_of(j * LANES, LANES), LANES)
        gradd[at, :] = over_tokens(hid[:, :, :, at], xall[1])

    write(4, gradd, dg_hbm)
    received(yl[0])
    input_slopes(0)
    scatter_core(1, 0)
    scatter_x(1, 0)
    fz_o = scatter_z(0)
    received(yl[1])
    input_slopes(1)
    scatter_core(1, 1)
    scatter_x(1, 1)

    @pl.loop(0, CHUNKS // 2)
    def _(j):
        at = pl.ds(pl.multiple_of(j * 2 * LANES, 2 * LANES), 2 * LANES)
        grads = dot(acts_t[at, :], slope[...].reshape(2 * HALF, 2 * HID), ((1,), (0,)))
        gradg[at, :] = grads[:, 0:HID].astype(BF16)
        gradu[at, :] = grads[:, HID : 2 * HID].astype(BF16)

    write(2, gradg, gg_hbm)
    write(3, gradu, ug_hbm)
    fz_i = scatter_z(1)
    finish(0, fz_o)
    finish(1, fz_i)
    for k in range(2):
        for i in range(NX):
            core_copy(k, i).wait_send()
        for order in range(2):
            for i in range(NX - 1):
                x_copy(k, order, i).wait_send()
    for copy in started:
        if all(copy is not other for other in gathers):
            copy.wait_send()
    for copy in stores:
        copy.wait()


def store(*refs):
    given, results, held = refs[0:5], refs[5:10], refs[10:15]
    sems = refs[15]
    copies = []
    for i in range(5):
        copies.append(
            (
                pltpu.make_async_copy(given[i], held[i], sems.at[0, i]),
                pltpu.make_async_copy(held[i], results[i], sems.at[1, i]),
            )
        )
        copies[i][0].start()
    for read, write in copies:
        read.wait()
        write.start()
    for _, write in copies:
        write.wait()


def body(activations, gate_weight, up_weight, down_weight, output_cotangent):
    hbm = pl.BlockSpec(memory_space=pltpu.HBM)
    dma = pltpu.SemaphoreType.DMA
    small = jax.ShapeDtypeStruct((OWN, WIDTH), BF16)
    tall = jax.ShapeDtypeStruct((WIDTH, HID), BF16)
    scratch = [
        pltpu.VMEM((2, OWN, WIDTH), BF16),
        pltpu.VMEM((WIDTH, 2 * HID), BF16),
        pltpu.VMEM((HID, WIDTH), BF16),
        pltpu.VMEM((WIDTH, 2 * HALF), BF16),
        pltpu.VMEM((2, 2, NX, NZ, OWN * CHUNKS, LANES), BF16),
        pltpu.VMEM((2, 2, NX, BLOCK, WIDTH), BF16),
        pltpu.VMEM((3, 2, NY, BLOCK, HID), BF16),
        pltpu.VMEM((3, 2, NY - 1, BLOCK, HID), BF16),
        pltpu.VMEM((3, 2, BLOCK, HID), BF16),
        pltpu.VMEM((3, 2, BLOCK, HID), BF16),
        pltpu.VMEM((2, 2, BLOCK, HID), F32),
        pltpu.VMEM((2, NY, BLOCK, HID), BF16),
        pltpu.VMEM((2, NY, BLOCK, 2 * HID), BF16),
        pltpu.VMEM((2, 2, NX, BLOCK, WIDTH), BF16),
        pltpu.VMEM((2, NX, BLOCK, WIDTH), BF16),
        pltpu.VMEM((2, NX, NZ, OWN * CHUNKS, LANES), BF16),
        pltpu.VMEM((2, NX - 1, NZ, OWN * CHUNKS, LANES), BF16),
        pltpu.VMEM((2, NZ, OWN * CHUNKS, LANES), BF16),
        pltpu.VMEM((2, NZ - 1, OWN * CHUNKS, LANES), BF16),
        pltpu.VMEM((2, OWN, WIDTH), BF16),
        pltpu.VMEM((WIDTH, HID), BF16),
        pltpu.VMEM((WIDTH, HID), BF16),
        pltpu.VMEM((HID, WIDTH), BF16),
        dma((5,)),
        dma((5,)),
    ]
    for shape in (
        (2, NZ - 1), (2, 2, NX - 1), (2, 2, NX), (3, 2, NY - 1), (3, 2),
        (2, NY - 1), (2, NY - 1), (2, NX), (2, 2, NX - 1), (2, NZ - 1),
    ):
        scratch += [dma(shape), dma(shape)]
    shapes = (small, small, tall, tall, jax.ShapeDtypeStruct((HID, WIDTH), BF16))
    results = pl.pallas_call(
        kernel,
        out_shape=shapes,
        in_specs=[hbm] * 5,
        out_specs=(hbm,) * 5,
        scratch_shapes=scratch,
        compiler_params=pltpu.CompilerParams(
            collective_id=0, has_side_effects=True, vmem_limit_bytes=61 << 20
        ),
    )(activations, output_cotangent, gate_weight, up_weight, down_weight)
    return pl.pallas_call(
        store,
        out_shape=shapes,
        in_specs=[hbm] * 5,
        out_specs=(hbm,) * 5,
        scratch_shapes=[pltpu.VMEM(s.shape, s.dtype) for s in shapes] + [dma((2, 5))],
    )(*results)


def solution(mesh):
    in_specs = (
        P(("dp", "col"), "row"),
        P("row", ("dp", "col")),
        P("row", ("dp", "col")),
        P(("dp", "col"), "row"),
        P(("dp", "col"), "row"),
    )
    out_specs = (
        P(("dp", "col"), "row"),
        P(("dp", "col"), "row"),
        P("row", ("dp", "col")),
        P("row", ("dp", "col")),
        P(("dp", "col"), "row"),
    )
    return jax.shard_map(body, mesh=mesh, in_specs=in_specs, out_specs=out_specs, check_vma=False)
```

```python
import jax
import jax.numpy as jnp
from jax import lax
from jax.experimental import pallas as pl
from jax.experimental.pallas import tpu as pltpu
from jax.sharding import PartitionSpec as P

MESH = pl.DeviceIdType.MESH
F32 = jnp.float32
BF16 = jnp.bfloat16
LANES = 128
OWN = 6
NX, NY, NZ = 4, 4, 8
BLOCK = OWN * NZ
HALF = NX * BLOCK
WIDTH = 1024
HID = 384
CHUNKS = WIDTH // LANES


def dot(left, right, dims):
    return lax.dot_general(left, right, (dims, ((), ())), preferred_element_type=F32)


def over_tokens(left, right):
    left, right = (v.reshape(2 * HALF, v.shape[-1]) for v in (left, right))
    return dot(left, right, ((0,), (0,))).astype(BF16)


def kernel(
    act_hbm, cot_hbm, gw_hbm, uw_hbm, dw_hbm,
    out_hbm, inp_hbm, gg_hbm, ug_hbm, dg_hbm,
    mine, wgu, wd, acts_t, xfine, xall, terms, trecv, tsend, tfar, sums,
    hid, slope, part, crecv, xsend, xrecv, zsend, zrecv, rows_out, gradg, gradu, gradd, wsem, osem,
    z_s, z_r, x_s, x_r, c_s, c_r, y_s, y_r, e_s, e_r,
    yh_s, yh_r, yl_s, yl_r, fc_s, fc_r, fx_s, fx_r, fz_s, fz_r,
):
    dp, row, zl = lax.axis_index("dp"), lax.axis_index("row"), lax.axis_index("col")
    x, c = dp // 2, lax.rem(dp, 2)
    y, zh = row // 2, lax.rem(row, 2)

    sib = {"dp": x * 2 + 1 - c}
    far = {"row": y * 2 + 1 - zh}

    half = zl // 4

    def xpos(i):
        return lax.rem(x + i, NX)

    def ypos(i):
        return lax.rem(y + i, NY)

    def zpos(m):
        place = 0
        for bit in (4, 2, 1):
            mine_ = lax.rem(zl // bit, 2)
            place = place + bit * (1 - mine_ if m & bit else mine_)
        return place

    def fours(order):
        return pl.ds(4 * (half if order == 0 else 1 - half), 4)

    def xdev(i):
        return {"dp": xpos(i) * 2 + c}

    def ydev(i):
        return {"row": ypos(i) * 2 + zh}

    def zdev(m):
        return {"col": zpos(m)}

    barrier = pltpu.get_barrier_semaphore()
    peers = [far] + [zdev(m) for m in range(NZ - 1, 0, -1)]
    peers += [ydev(i) for i in range(1, NY)]
    peers += [xdev(i) for i in range(1, NX)] + [sib]
    for peer in peers:
        pl.semaphore_signal(barrier, inc=1, device_id=peer, device_id_type=MESH)

    loads = [
        pltpu.make_async_copy(act_hbm, mine.at[0], wsem.at[3]),
        pltpu.make_async_copy(cot_hbm, mine.at[1], wsem.at[4]),
        pltpu.make_async_copy(gw_hbm, wgu.at[:, 0:HID], wsem.at[0]),
        pltpu.make_async_copy(uw_hbm, wgu.at[:, HID : 2 * HID], wsem.at[1]),
        pltpu.make_async_copy(dw_hbm, wd, wsem.at[2]),
    ]
    for load in loads[0:2]:
        load.start()

    def to_fine(value):
        return value.reshape(value.shape[0] * CHUNKS, LANES)

    def from_fine(value):
        return value.reshape(value.shape[0] // CHUNKS, WIDTH)

    for kind in range(2):
        loads[kind].wait()
        xfine[kind, c, x, zl] = to_fine(mine[kind].astype(F32)).astype(BF16)

    pl.semaphore_wait(barrier, len(peers))

    started = []

    def send(src, dst, s, r, device):
        copy = pltpu.make_async_remote_copy(
            src_ref=src, dst_ref=dst, send_sem=s, recv_sem=r, device_id=device, device_id_type=MESH
        )
        copy.start()
        started.append(copy)
        return copy

    def z_gather(kind):
        piece = xfine.at[kind, c, x, zl]
        copies = {}
        for m in (7, 6, 5, 4, 3, 2, 1):
            copies[m] = send(piece, piece, z_s.at[kind, m - 1], z_r.at[kind, m - 1], zdev(m))
        return copies

    def forward(kind, where, order, i):
        block = xfine.at[kind, c, where, fours(order)]
        return send(block, block, c_s.at[kind, order, i], c_r.at[kind, order, i], sib)

    def x_gather(kind, copies):
        xs, cs = [], []
        for order in range(2):
            for m in ((1, 2, 3), (4, 5, 6, 7))[order]:
                copies[m].wait_recv()
            block = xfine.at[kind, c, x, fours(order)]
            for i in range(NX - 1):
                sems = x_s.at[kind, order, i], x_r.at[kind, order, i]
                xs.append(send(block, block, *sems, xdev(i + 1)))
            cs.append(forward(kind, x, order, 0))
        return xs, cs

    def lay_out(kind, t, where):
        pieces = xfine[kind, t, where].reshape(BLOCK * CHUNKS, LANES)
        xall[kind, t, where] = from_fine(pieces.astype(F32)).astype(BF16)

    def pass_on(kind, xs, cs):
        lay_out(kind, c, x)
        for order in range(2):
            for i in (0, 2, 1):
                where = lax.rem(x + NX - i - 1, NX)
                xs[order * (NX - 1) + i].wait_recv()
                cs.append(forward(kind, where, order, i + 1))
                if order == 1:
                    lay_out(kind, c, where)

    def from_sibling(kind, cs):
        received(cs)
        for where in range(NX):
            lay_out(kind, 1 - c, where)

    def y_scatter(q, k):
        return [
            send(
                terms.at[q, k, ypos(i + 1)], trecv.at[q, k, i],
                y_s.at[q, k, i], y_r.at[q, k, i], ydev(i + 1),
            )
            for i in range(NY - 1)
        ]

    def y_sum(q, k, copies):
        total = terms[q, k, y].astype(F32)
        for i in (0, 2, 1):
            copies[i].wait_recv()
            total = total + trecv[q, k, i].astype(F32)
        tsend[q, k] = total.astype(BF16)
        return send(tsend.at[q, k], tfar.at[q, k], e_s.at[q, k], e_r.at[q, k], far)

    def whole(q, k):
        return tsend[q, k].astype(F32) + tfar[q, k].astype(F32)

    def y_gather(t, k, buf, s, r):
        return [
            send(buf.at[t, y], buf.at[t, y], s.at[k, i], r.at[k, i], ydev(i + 1))
            for i in range(NY - 1)
        ]

    stores = []

    def write(i, src, dst):
        stores.append(pltpu.make_async_copy(src, dst, osem.at[i]))
        stores[-1].start()

    def received(copies):
        for copy in copies:
            copy.wait_recv()

    def core_copy(k, i):
        where = xpos(i)
        return pltpu.make_async_remote_copy(
            src_ref=part.at[k, 1 - c, where], dst_ref=crecv.at[k, where], send_sem=fc_s.at[k, i],
            recv_sem=fc_r.at[k, i], device_id=sib, device_id_type=MESH,
        )

    def x_copy(k, order, i):
        at = fours(1 - order)
        return pltpu.make_async_remote_copy(
            src_ref=xsend.at[k, xpos(i + 1), at], dst_ref=xrecv.at[k, i, at],
            send_sem=fx_s.at[k, order, i], recv_sem=fx_r.at[k, order, i],
            device_id=xdev(i + 1), device_id_type=MESH,
        )

    def scatter_core(k, t):
        @pl.when(c == 1 - t)
        def _():
            for i in (2, 1, 3, 0):
                core_copy(k, i).start()

    def scatter_x(k, t):
        @pl.when(c == t)
        def _():
            for i in (2, 1, 3, 0):
                where = xpos(i)
                core_copy(k, i).wait_recv()
                total = part[k, c, where].astype(F32) + crecv[k, where].astype(F32)
                xsend[k, where] = to_fine(total).astype(BF16).reshape(NZ, OWN * CHUNKS, LANES)
                if i > 0:
                    for order in range(2):
                        x_copy(k, order, i - 1).start()

    def scatter_z(k):
        copies = []
        for order in range(2):
            at = fours(1 - order)
            total = xsend[k, x, at].astype(F32)
            for i in (0, 2, 1):
                x_copy(k, order, i).wait_recv()
                total = total + xrecv[k, i, at].astype(F32)
            zsend[k, at] = total.astype(BF16)
            for m in ((7, 6, 5, 4), (3, 2, 1))[order]:
                sems = fz_s.at[k, m - 1], fz_r.at[k, m - 1]
                copies.append(send(zsend.at[k, zpos(m)], zrecv.at[k, m - 1], *sems, zdev(m)))
        return copies

    def finish(k, copies):
        total = zsend[k, zl].astype(F32)
        received(copies)
        for i in range(NZ - 1):
            total = total + zrecv[k, i].astype(F32)
        rows_out[k] = from_fine(total).astype(BF16)
        write(k, rows_out.at[k], (out_hbm, inp_hbm)[k])

    def gate_up_terms(t, k):
        both = dot(xall[0, t].reshape(HALF, WIDTH), wgu[...], ((1,), (0,))).astype(BF16)
        copies = []
        for q in range(2):
            terms[q, k] = both[:, q * HID : (q + 1) * HID].reshape(NY, BLOCK, HID)
            copies.append(y_scatter(q, k))
        return copies

    def slope_terms(t):
        terms[2, t] = (
            dot(xall[1, t].reshape(HALF, WIDTH), wd[...], ((1,), (1,)))
            .astype(BF16)
            .reshape(NY, BLOCK, HID)
        )
        return y_scatter(2, t)

    def hidden_units(t, k):
        gate, up = whole(0, k), whole(1, k)
        sums[0, t], sums[1, t] = gate, up
        hid[t, y] = (gate * jax.nn.sigmoid(gate) * up).astype(BF16)
        return y_gather(t, k, hid, yh_s, yh_r)

    def slope_pair(t):
        gate, up, ds = sums[0, t], sums[1, t], whole(2, t)
        s = jax.nn.sigmoid(gate)
        slope[t, y, :, 0:HID] = (ds * up * s * (1.0 + gate * (1.0 - s))).astype(BF16)
        slope[t, y, :, HID : 2 * HID] = (ds * gate * s).astype(BF16)
        return y_gather(t, t, slope, yl_s, yl_r)

    def outputs(t):
        total = dot(hid[t].reshape(HALF, HID), wd[...], ((1,), (0,)))
        part[0, t] = total.astype(BF16).reshape(NX, BLOCK, WIDTH)

    def input_slopes(t):
        total = dot(slope[t].reshape(HALF, 2 * HID), wgu[...], ((1,), (1,)))
        part[1, t] = total.astype(BF16).reshape(NX, BLOCK, WIDTH)

    az = z_gather(0)
    for load in loads[2:5]:
        load.start()
    ax, ac = x_gather(0, az)
    cz = z_gather(1)
    pass_on(0, ax, ac)
    loads[2].wait()
    loads[3].wait()
    yg = [gate_up_terms(c, 0)]
    from_sibling(0, ac)
    yg.append(gate_up_terms(1 - c, 1))
    cx, cc = x_gather(1, cz)
    eg = [y_sum(0, 0, yg[0][0]), y_sum(1, 0, yg[0][1])]
    pass_on(1, cx, cc)
    loads[4].wait()
    eg.append(y_sum(0, 1, yg[1][0]))
    from_sibling(1, cc)
    ys = [slope_terms(t) for t in range(2)]
    eg.append(y_sum(1, 1, yg[1][1]))
    gathers = [copy for copy in started if all(copy is not other for other in eg)]
    es = [y_sum(2, t, ys[t]) for t in range(2)]

    @pl.loop(0, CHUNKS)
    def _(j):
        at = pl.ds(pl.multiple_of(j * LANES, LANES), LANES)
        acts_t[at, :] = xall[0, :, :, :, at].reshape(2 * HALF, LANES).T

    for copy in gathers:
        copy.wait_send()

    received(eg[0:2])
    yh = hidden_units(c, 0)
    received(eg[2:4])
    yh += hidden_units(1 - c, 1)
    received(es[0:1])
    yl = [slope_pair(0)]
    received(yh)
    for t in range(2):
        outputs(t)
        scatter_core(0, t)
    for t in range(2):
        scatter_x(0, t)
    received(es[1:2])
    yl.append(slope_pair(1))

    @pl.loop(0, HID // LANES)
    def _(j):
        at = pl.ds(pl.multiple_of(j * LANES, LANES), LANES)
        gradd[at, :] = over_tokens(hid[:, :, :, at], xall[1])

    write(4, gradd, dg_hbm)
    received(yl[0])
    input_slopes(0)
    scatter_core(1, 0)
    scatter_x(1, 0)
    fz_o = scatter_z(0)
    received(yl[1])
    input_slopes(1)
    scatter_core(1, 1)
    scatter_x(1, 1)

    fz_i = scatter_z(1)

    @pl.loop(0, CHUNKS // 2)
    def _(j):
        at = pl.ds(pl.multiple_of(j * 2 * LANES, 2 * LANES), 2 * LANES)
        grads = dot(acts_t[at, :], slope[...].reshape(2 * HALF, 2 * HID), ((1,), (0,)))
        gradg[at, :] = grads[:, 0:HID].astype(BF16)
        gradu[at, :] = grads[:, HID : 2 * HID].astype(BF16)

    write(2, gradg, gg_hbm)
    write(3, gradu, ug_hbm)
    finish(0, fz_o)
    for k in range(2):
        for i in range(NX):
            core_copy(k, i).wait_send()
        for order in range(2):
            for i in range(NX - 1):
                x_copy(k, order, i).wait_send()
    for copy in started:
        if all(copy is not other for other in gathers):
            copy.wait_send()
    finish(1, fz_i)
    for copy in stores:
        copy.wait()


def store(*refs):
    given, results, held = refs[0:5], refs[5:10], refs[10:15]
    sems = refs[15]
    copies = []
    for i in range(5):
        copies.append(
            (
                pltpu.make_async_copy(given[i], held[i], sems.at[0, i]),
                pltpu.make_async_copy(held[i], results[i], sems.at[1, i]),
            )
        )
        copies[i][0].start()
    for read, write in copies:
        read.wait()
        write.start()
    for _, write in copies:
        write.wait()


def body(activations, gate_weight, up_weight, down_weight, output_cotangent):
    hbm = pl.BlockSpec(memory_space=pltpu.HBM)
    dma = pltpu.SemaphoreType.DMA
    small = jax.ShapeDtypeStruct((OWN, WIDTH), BF16)
    tall = jax.ShapeDtypeStruct((WIDTH, HID), BF16)
    scratch = [
        pltpu.VMEM((2, OWN, WIDTH), BF16),
        pltpu.VMEM((WIDTH, 2 * HID), BF16),
        pltpu.VMEM((HID, WIDTH), BF16),
        pltpu.VMEM((WIDTH, 2 * HALF), BF16),
        pltpu.VMEM((2, 2, NX, NZ, OWN * CHUNKS, LANES), BF16),
        pltpu.VMEM((2, 2, NX, BLOCK, WIDTH), BF16),
        pltpu.VMEM((3, 2, NY, BLOCK, HID), BF16),
        pltpu.VMEM((3, 2, NY - 1, BLOCK, HID), BF16),
        pltpu.VMEM((3, 2, BLOCK, HID), BF16),
        pltpu.VMEM((3, 2, BLOCK, HID), BF16),
        pltpu.VMEM((2, 2, BLOCK, HID), F32),
        pltpu.VMEM((2, NY, BLOCK, HID), BF16),
        pltpu.VMEM((2, NY, BLOCK, 2 * HID), BF16),
        pltpu.VMEM((2, 2, NX, BLOCK, WIDTH), BF16),
        pltpu.VMEM((2, NX, BLOCK, WIDTH), BF16),
        pltpu.VMEM((2, NX, NZ, OWN * CHUNKS, LANES), BF16),
        pltpu.VMEM((2, NX - 1, NZ, OWN * CHUNKS, LANES), BF16),
        pltpu.VMEM((2, NZ, OWN * CHUNKS, LANES), BF16),
        pltpu.VMEM((2, NZ - 1, OWN * CHUNKS, LANES), BF16),
        pltpu.VMEM((2, OWN, WIDTH), BF16),
        pltpu.VMEM((WIDTH, HID), BF16),
        pltpu.VMEM((WIDTH, HID), BF16),
        pltpu.VMEM((HID, WIDTH), BF16),
        dma((5,)),
        dma((5,)),
    ]
    for shape in (
        (2, NZ - 1), (2, 2, NX - 1), (2, 2, NX), (3, 2, NY - 1), (3, 2),
        (2, NY - 1), (2, NY - 1), (2, NX), (2, 2, NX - 1), (2, NZ - 1),
    ):
        scratch += [dma(shape), dma(shape)]
    shapes = (small, small, tall, tall, jax.ShapeDtypeStruct((HID, WIDTH), BF16))
    results = pl.pallas_call(
        kernel,
        out_shape=shapes,
        in_specs=[hbm] * 5,
        out_specs=(hbm,) * 5,
        scratch_shapes=scratch,
        compiler_params=pltpu.CompilerParams(
            collective_id=0, has_side_effects=True, vmem_limit_bytes=61 << 20
        ),
    )(activations, output_cotangent, gate_weight, up_weight, down_weight)
    return pl.pallas_call(
        store,
        out_shape=shapes,
        in_specs=[hbm] * 5,
        out_specs=(hbm,) * 5,
        scratch_shapes=[pltpu.VMEM(s.shape, s.dtype) for s in shapes] + [dma((2, 5))],
    )(*results)


def solution(mesh):
    in_specs = (
        P(("dp", "col"), "row"),
        P("row", ("dp", "col")),
        P("row", ("dp", "col")),
        P(("dp", "col"), "row"),
        P(("dp", "col"), "row"),
    )
    out_specs = (
        P(("dp", "col"), "row"),
        P(("dp", "col"), "row"),
        P("row", ("dp", "col")),
        P("row", ("dp", "col")),
        P(("dp", "col"), "row"),
    )
    return jax.shard_map(body, mesh=mesh, in_specs=in_specs, out_specs=out_specs, check_vma=False)
```
